1024 devices in a mesh: dp: 64 (over z, core), expert: 16 (over x, y).
Axes of the slice: x: 4, y: 4, z: 32, core: 2. Of those that a mesh axis runs over, the one named last changes fastest.
Arguments:
- tokens: bfloat16 [4096, 4096], P('dp', 'expert'), may hold values from -6 to 6
- grad_out: bfloat16 [4096, 4096], P('dp', 'expert'), may hold values from -6 to 6
- picked: int32 [64, 16, 3], P('dp'), may hold values from 0 to 63, as said below
- pick_counts: int32 [64, 16], P('dp'), may hold values from 1 to 3, as said below
- router_weights: float32 [64, 16, 3], P('dp'), may hold values from 0.1 to 1
- saved_gate: bfloat16 [16, 192, 2048], P('expert', 'dp'), may hold values from -6 to 6
- saved_up: bfloat16 [16, 192, 2048], P('expert', 'dp'), may hold values from -6 to 6
- w_gate: bfloat16 [16, 4096, 2048], P('expert', 'dp'), may hold values from -0.09375 to 0.09375
- w_up: bfloat16 [16, 4096, 2048], P('expert', 'dp'), may hold values from -0.09375 to 0.09375
- w_down: bfloat16 [16, 2048, 4096], P('expert', None, 'dp'), may hold values from -0.125 to 0.125
Outputs:
- token_grad: bfloat16 [4096, 4096], P('dp', 'expert')
- w_gate_grad: float32 [16, 4096, 2048], P('expert', 'dp')
- w_up_grad: float32 [16, 4096, 2048], P('expert', 'dp')
- w_down_grad: float32 [16, 2048, 4096], P('expert', None, 'dp')
The draws below stay inside these ranges and needn't reach their ends.
Inputs may be any that keep to these rules, and one draw needn't show every extreme that they name: `picked`: the 3 entries for one shard and one expert are distinct token numbers of that shard; only the first pick_counts of them are picks. `pick_counts`: in every draw some expert has 3 picks from every shard, and every shard gives 3 picks to some expert.
All inputs are finite; a program needn't handle non-finite values.
Results may differ from the reference program's by a relative error of at most 0.0067.
Values may be sent and summed in bfloat16 or wider, within the bound.
No kernel may reach another device: no remote copies, remote signals or barrier semaphores. Data moves between devices by JAX's collectives and lax.ppermute only.
A program may use at most 32 MiB of HBM per device.

```python
import jax
import jax.numpy as jnp
from jax import lax

D = 4096
FF = 2048
TOK_DP = 64
EXPERTS = 16
SHARDS = 64
CAP = 3
SLOTS = 192
TOKENS = 4096


def draw_picked(key, part):
    key = jax.random.fold_in(key, 17)
    keys = jax.random.split(key, SHARDS * EXPERTS)
    orders = jax.vmap(lambda single: jax.random.permutation(single, TOK_DP))(keys)
    return orders[:, :CAP].reshape(SHARDS, EXPERTS, CAP).astype(jnp.int32)


def draw_pick_counts(key, part):
    key = jax.random.fold_in(key, 11)
    first, second, third = jax.random.split(key, 3)
    base_counts = jax.random.randint(first, (SHARDS, EXPERTS), 1, CAP + 1)
    full_expert = jax.random.randint(second, (), 0, EXPERTS)
    extra_expert = jax.random.randint(third, (SHARDS,), 0, EXPERTS)
    columns = jnp.arange(EXPERTS)
    forced = (columns[None, :] == full_expert) | (columns[None, :] == extra_expert[:, None])
    return jnp.where(forced, CAP, base_counts).astype(jnp.int32)


def block_levels(key, extent, shards, low, largest):
    level, own = 1.0, jax.random.fold_in(key, 6)
    for dim, parts in shards:
        draws = jnp.exp(jax.random.uniform(jax.random.fold_in(own, dim), (parts,), jnp.float32, low / len(shards), largest / len(shards)))
        level = level * jnp.repeat(draws, extent[dim] // parts).reshape([-1 if axis == dim else 1 for axis in range(len(extent))])
    return level


def scatter_about(key, shape, spread, bound, cuts=(), kind=jnp.bfloat16):
    entries = jax.random.normal(key, shape, jnp.float32) * spread
    if len(cuts) > 0:
        entries = block_levels(key, shape, cuts, -0.22, 0.18) * entries
    return jnp.clip(entries, min=-bound, max=bound).astype(kind)


def setup_inputs(seed: int = 0) -> dict:
    splits = jax.random.split(jax.random.key(seed), 11)
    tokens = scatter_about(splits[0], (TOKENS, D), 1.0, 6.0, ((0, 64), (1, 16)))
    grad_out = scatter_about(splits[1], (TOKENS, D), 1.0, 6.0, ((0, 64), (1, 16)))
    picked = draw_picked(jax.random.fold_in(splits[10], 71), 0)
    pick_counts = draw_pick_counts(jax.random.fold_in(splits[10], 71), 0)
    router_weights = jnp.clip(0.1 + 0.9 * jax.random.uniform(splits[4], (SHARDS, EXPERTS, CAP), jnp.float32) ** block_levels(splits[4], (SHARDS, EXPERTS, CAP), ((0, 64),), -0.2, 0.2), 0.1, 1.0)
    saved_gate = scatter_about(splits[5], (EXPERTS, SLOTS, FF), 1.0, 6.0, ((0, 16), (1, 64)))
    saved_up = scatter_about(splits[6], (EXPERTS, SLOTS, FF), 1.0, 6.0, ((0, 16), (1, 64)))
    w_gate = scatter_about(splits[7], (EXPERTS, D, FF), D ** -0.5, 0.09375, ((0, 16), (1, 64)))
    w_up = scatter_about(splits[8], (EXPERTS, D, FF), D ** -0.5, 0.09375, ((0, 16), (1, 64)))
    w_down = scatter_about(splits[9], (EXPERTS, FF, D), FF ** -0.5, 0.125, ((0, 16), (2, 64)))
    return dict(tokens=tokens, grad_out=grad_out, picked=picked, pick_counts=pick_counts, router_weights=router_weights, saved_gate=saved_gate, saved_up=saved_up, w_gate=w_gate, w_up=w_up, w_down=w_down)


def hidden_terms(hidden_grad, gate_value, up_value):
    gate_float = gate_value.astype(jnp.float32)
    up_float = up_value.astype(jnp.float32)
    hidden_float = hidden_grad.astype(jnp.float32)
    sigmoid_gate = jax.nn.sigmoid(gate_float)
    activated = (gate_float * sigmoid_gate * up_float).astype(jnp.bfloat16)
    gate_grad = (hidden_float * up_float * sigmoid_gate * (1.0 + gate_float * (1.0 - sigmoid_gate))).astype(jnp.bfloat16)
    up_grad = (hidden_float * gate_float * sigmoid_gate).astype(jnp.bfloat16)
    return activated, gate_grad, up_grad


def one_expert(operands):
    picked_in, sent, gate_value, up_value, gate_weight, up_weight, down_weight = operands
    hidden_grad = jnp.dot(sent, down_weight.T, preferred_element_type=jnp.float32).astype(jnp.bfloat16)
    activated, gate_grad, up_grad = hidden_terms(hidden_grad, gate_value, up_value)
    gate_total = jnp.dot(picked_in.T, gate_grad, preferred_element_type=jnp.float32)
    up_total = jnp.dot(picked_in.T, up_grad, preferred_element_type=jnp.float32)
    down_total = jnp.dot(activated.T, sent, preferred_element_type=jnp.float32)
    slot_grad = (jnp.dot(gate_grad, gate_weight.T, preferred_element_type=jnp.float32)
                 + jnp.dot(up_grad, up_weight.T, preferred_element_type=jnp.float32)).astype(jnp.bfloat16)
    return gate_total, up_total, down_total, slot_grad


def reference(tokens, grad_out, picked, pick_counts, router_weights, saved_gate, saved_up, w_gate, w_up, w_down):
    slot_index = jnp.arange(CAP, dtype=jnp.int32)
    live_slots = slot_index[None, None, :] < pick_counts[:, :, None]
    offsets = (jnp.arange(SHARDS, dtype=jnp.int32) * TOK_DP)[:, None, None]
    token_index = jnp.transpose(picked + offsets, (1, 0, 2)).reshape(EXPERTS, SLOTS).astype(jnp.int32)
    scales = jnp.where(live_slots, router_weights, jnp.float32(0.0))
    scales = jnp.transpose(scales, (1, 0, 2)).reshape(EXPERTS, SLOTS)
    picked_in = tokens[token_index]
    sent = (grad_out[token_index].astype(jnp.float32) * scales[:, :, None]).astype(jnp.bfloat16)
    gate_total, up_total, down_total, slot_grad = lax.map(
        one_expert, (picked_in, sent, saved_gate, saved_up, w_gate, w_up, w_down))
    summed = jnp.zeros((TOKENS, D), jnp.float32).at[token_index.reshape(-1)].add(
        slot_grad.reshape(EXPERTS * SLOTS, D).astype(jnp.float32))
    return summed.astype(jnp.bfloat16), gate_total, up_total, down_total
```

```python
import functools

import jax
import jax.numpy as jnp
from jax import lax
from jax.experimental import pallas as pl
from jax.experimental.pallas import tpu as pltpu
from jax.sharding import Mesh
from jax.sharding import PartitionSpec as P

BF16 = jnp.bfloat16
F32 = jnp.float32
CAP = 3
HALF = 64
LANES = 128
NT = (((1,), (1,)), ((), ()))
TN = (((0,), (0,)), ((), ()))
VMEM = pl.BlockSpec(memory_space=pltpu.VMEM)
SMEM = pl.BlockSpec(memory_space=pltpu.SMEM)


def call(body, outs, ins, scratch=(), cost=None):
    return pl.pallas_call(
        body,
        out_shape=outs,
        in_specs=ins,
        out_specs=jax.tree.map(lambda _: VMEM, outs),
        scratch_shapes=list(scratch),
        compiler_params=pltpu.CompilerParams(vmem_limit_bytes=40 * 1024 * 1024),
        cost_estimate=cost,
    )


def struct(*shape, dtype=BF16):
    return jax.ShapeDtypeStruct(shape, dtype)


def weave(first, second):
    low = lax.broadcasted_iota(jnp.int32, first.shape, 1) < HALF
    return (
        jnp.where(low, first, pltpu.roll(second, HALF, 1)),
        jnp.where(low, pltpu.roll(first, HALF, 1), second),
    )


def pick_body(picked_ref, counts_ref, weights_ref, tokens_ref, grads_ref, out_ref, wide_in, wide_out, rows):
    wide_in[...] = tokens_ref[...].astype(F32)
    wide_out[...] = grads_ref[...].astype(F32)
    rows[...] = jnp.zeros_like(rows)
    for expert in range(out_ref.shape[0]):
        for c in range(CAP):
            token = picked_ref[c, expert]
            scale = jnp.where(c < counts_ref[0, expert], weights_ref[c, expert], 0.0)
            rows[pl.ds(8 * expert + c, 1), :] = wide_out[pl.ds(token, 1), :] * scale
            rows[pl.ds(8 * expert + 4 + c, 1), :] = wide_in[pl.ds(token, 1), :]
    out_ref[...] = rows[...].reshape(out_ref.shape).astype(BF16)


def turn_body(down_ref, gate_ref, up_ref, out_ref):
    for pair in range(down_ref.shape[1] // LANES):
        columns = slice(pair * LANES, (pair + 1) * LANES)
        block = down_ref[:, columns].astype(F32)
        one, two = weave(block[:32], block[32:])
        out_ref[2 * pair, 0:32, :] = one.astype(BF16)
        out_ref[2 * pair + 1, 0:32, :] = two.astype(BF16)
        one, two = weave(gate_ref[:, columns].astype(F32), up_ref[:, columns].astype(F32))
        blank = jnp.zeros((8 - CAP, LANES), F32)
        out_ref[2 * pair, 32:40, :] = jnp.concatenate([one, blank]).astype(BF16)
        out_ref[2 * pair + 1, 32:40, :] = jnp.concatenate([two, blank]).astype(BF16)


def weave_body(gate_ref, up_ref, out_ref):
    for pair in range(gate_ref.shape[1] // LANES):
        columns = slice(pair * LANES, (pair + 1) * LANES)
        one, two = weave(gate_ref[:, columns].astype(F32), up_ref[:, columns].astype(F32))
        out_ref[:, 2 * pair * LANES : (2 * pair + 1) * LANES] = one.astype(BF16)
        out_ref[:, (2 * pair + 1) * LANES : (2 * pair + 2) * LANES] = two.astype(BF16)


def row_body(blocks_ref, out_ref):
    width = blocks_ref.shape[2]
    for f in range(blocks_ref.shape[0]):
        out_ref[0, :, f * width : (f + 1) * width] = blocks_ref[f, 0:CAP, :]


def spread_body(core_ref, own_ref, other_ref, out_ref):
    first = core_ref[0] == 0
    for z in range(own_ref.shape[0]):
        own = own_ref[z, 0:32, :].astype(F32)
        other = other_ref[z, 0:32, :].astype(F32)
        zero, one = jnp.where(first, own, other), jnp.where(first, other, own)
        parts = [zero, pltpu.roll(zero, HALF, 1), one, pltpu.roll(one, HALF, 1)]
        out_ref[z * LANES : (z + 1) * LANES, :] = jnp.concatenate(parts).astype(BF16)


def hidden_body(sent_ref, down_ref, saved_ref, out_ref):
    hidden = jnp.dot(sent_ref[...], down_ref[...], preferred_element_type=F32)
    hidden = hidden.astype(BF16).astype(F32)
    saved = saved_ref[...].astype(F32)
    a, b = saved, pltpu.roll(saved, HALF, 1)
    q = jax.nn.sigmoid(a)
    gate_grad = hidden * b * q * (1.0 + a * (1.0 - q))
    up_grad = hidden * a * q
    low = lax.broadcasted_iota(jnp.int32, hidden.shape, 1) < HALF
    both = jnp.where(low, gate_grad, pltpu.roll(up_grad, HALF, 1))
    out_ref[...] = both.T.astype(BF16)


def slot_body(core_ref, grads_ref, own_ref, other_ref, blocks_ref, out_ref):
    grads = grads_ref[...]
    own = jnp.dot(own_ref[...], grads, preferred_element_type=F32)
    other = jnp.dot(other_ref[...], grads, preferred_element_type=F32)
    first = core_ref[0] == 0
    whole = jnp.concatenate([jnp.where(first, own, other), jnp.where(first, other, own)]).astype(BF16)
    chips = out_ref.shape[0]
    row = lax.broadcasted_iota(jnp.int32, (8 * chips, CAP * chips), 0)
    slot = lax.broadcasted_iota(jnp.int32, (8 * chips, CAP * chips), 1)
    place = (row // 8 * CAP + row % 8 == slot) & (row % 8 < CAP)
    placed = lax.dot_general(place.astype(BF16), whole, NT, preferred_element_type=F32)
    lower = lax.broadcasted_iota(jnp.int32, (8, LANES), 0) >= 4
    for z in range(chips):
        rows = blocks_ref[z // 2, :, z % 2 * LANES : (z % 2 + 1) * LANES].astype(F32)
        out_ref[z] = jnp.where(lower, rows, placed[8 * z : 8 * z + 8]).astype(BF16)


def weight_body(in_own, in_other, own_ref, other_ref, gate_ref, up_ref):
    chips = own_ref.shape[0]
    for pair in range(chips // 2):
        columns = slice(pair * LANES, (pair + 1) * LANES)
        for start, out_ref in ((0, gate_ref), (HALF, up_ref)):
            total = None
            for rows, grads in ((in_own, own_ref), (in_other, other_ref)):
                block = jnp.concatenate(
                    [grads[2 * pair, start : start + HALF, :], grads[2 * pair + 1, start : start + HALF, :]]
                )
                part = lax.dot_general(rows[...], block, NT, preferred_element_type=F32)
                total = part if total is None else total + part
            out_ref[:, columns] = total


def down_body(sent_ref, act_ref, out_ref):
    out_ref[...] = lax.dot_general(sent_ref[...], act_ref[...], TN, preferred_element_type=F32)


def token_body(index_ref, rows_ref, out_ref):
    tokens = lax.broadcasted_iota(jnp.int32, (out_ref.shape[0], index_ref.shape[1]), 0)
    for half in range(2):
        owner = (tokens == index_ref[half : half + 1, :]).astype(BF16)
        total = jnp.dot(owner, rows_ref[...], preferred_element_type=F32)
        out_ref[:, half * LANES : (half + 1) * LANES] = total.astype(BF16)


def swap(x):
    return lax.ppermute(x, "core", [(0, 1), (1, 0)])


def local(chips, tokens, grad_out, picked, pick_counts, router_weights, saved_gate, saved_up, w_gate, w_up, w_down):
    experts = picked.shape[1]
    token_count, width = tokens.shape
    hidden = w_gate.shape[2]
    slots = CAP * chips
    core = lax.axis_index("core")
    core_word = core.astype(jnp.int32).reshape(1)
    gate_value, up_value = saved_gate[0], saved_up[0]
    picks = picked[0].T

    gate_float = gate_value.astype(F32)
    activated = gate_float * jax.nn.sigmoid(gate_float) * up_value.astype(F32)
    activated = jnp.pad(activated.astype(BF16), ((0, 1), (0, 0)))
    activated = lax.all_gather(activated, ("z", "core"), axis=0, tiled=False)

    turned = call(turn_body, struct(chips, 40, LANES), [VMEM] * 3)(w_down[0].T, gate_value, up_value)
    turned = lax.all_to_all(turned, "z", split_axis=0, concat_axis=0, tiled=True)

    woven = call(weave_body, struct(HALF, 2 * hidden), [VMEM] * 2)(w_gate[0], w_up[0])
    woven_other = swap(woven)

    outgoing = call(
        pick_body,
        struct(experts, 8, width),
        [SMEM] * 3 + [VMEM] * 2,
        scratch=(
            pltpu.VMEM((token_count, width), F32),
            pltpu.VMEM((token_count, width), F32),
            pltpu.VMEM((8 * experts, width), F32),
        ),
    )(picks, pick_counts, router_weights[0].T, tokens, grad_out)
    arrived = lax.all_to_all(outgoing, "expert", split_axis=0, concat_axis=0, tiled=True)
    sent = call(row_body, struct(1, CAP, experts * width), [VMEM])(arrived)
    sent = lax.all_gather(sent, "z", axis=0, tiled=True).reshape(slots, experts * width)

    turned_other = swap(turned[:, 0:32, :])
    down = call(spread_body, struct(experts * width, LANES), [SMEM, VMEM, VMEM])(core_word, turned, turned_other)
    saved = turned[:, 32 : 32 + CAP, :].reshape(slots, LANES)
    grads = call(hidden_body, struct(LANES, slots), [VMEM] * 3)(sent, down, saved)
    grads = lax.all_gather(grads[None], "z", axis=0, tiled=True)

    returned = call(slot_body, struct(chips, 8, LANES), [SMEM] + [VMEM] * 4)(
        core_word, grads.reshape(chips * LANES, slots), woven, woven_other, arrived
    )
    returned = lax.all_to_all(returned, "z", split_axis=0, concat_axis=0, tiled=True)
    back = lax.all_to_all(
        returned.reshape(experts, 16, LANES), "expert", split_axis=0, concat_axis=0, tiled=True
    )

    lane = jnp.arange(16 * experts, dtype=jnp.int32)
    index = jnp.repeat(jnp.pad(picked[0], ((0, 0), (0, 8 - CAP)), constant_values=-1), 2, axis=0).reshape(1, -1)
    index = jnp.where(lane[None, :] // 8 % 2 == jnp.arange(2)[:, None], index, -1)
    token_grad = call(token_body, struct(token_count, width), [VMEM] * 2)(
        index, back.reshape(16 * experts, LANES)
    )

    grads_other = swap(grads)
    chip_width = lax.dynamic_slice_in_dim(sent, lax.axis_index("z") * LANES, LANES, axis=1)

    def parts(x):
        kept = jnp.where(core == 0, x[:, :HALF], x[:, HALF:])
        given = jnp.where(core == 0, x[:, HALF:], x[:, :HALF])
        return kept, swap(given)

    sent_own, sent_other = parts(chip_width)
    both = jnp.stack([jnp.where(core == 0, sent_own, sent_other), jnp.where(core == 0, sent_other, sent_own)], axis=1)
    both = both.reshape(chips, CAP, 2, HALF).transpose(0, 2, 1, 3)
    both = jnp.pad(both, ((0, 0), (0, 0), (0, 1), (0, 0))).reshape(8 * chips, HALF)
    down_grad = call(down_body, struct(HALF, hidden, dtype=F32), [VMEM] * 2)(
        both, activated.reshape(8 * chips, hidden)
    )

    in_own, in_other = parts(returned[:, 4 : 4 + CAP, :].reshape(slots, LANES))
    gate_grad, up_grad = call(
        weight_body, (struct(HALF, hidden, dtype=F32), struct(HALF, hidden, dtype=F32)), [VMEM] * 4
    )(in_own.T, in_other.T, grads, grads_other)
    return (token_grad, gate_grad[None], up_grad[None], down_grad.T[None])


def solution(mesh):
    chips = mesh.shape["dp"] // 2
    fine = Mesh(mesh.devices.reshape(chips, 2, mesh.shape["expert"]), ("z", "core", "expert"))
    dp = ("z", "core")
    placed = (
        P(dp, "expert"),
        P(dp, "expert"),
        P(dp, None, None),
        P(dp, None),
        P(dp, None, None),
        P("expert", dp, None),
        P("expert", dp, None),
        P("expert", dp, None),
        P("expert", dp, None),
        P("expert", None, dp),
    )
    return jax.shard_map(
        functools.partial(local, chips),
        mesh=fine,
        in_specs=placed,
        out_specs=(
            P(dp, "expert"),
            P("expert", dp, None),
            P("expert", dp, None),
            P("expert", None, dp),
        ),
        check_vma=False,
    )
```

```python
import functools

import jax
import jax.numpy as jnp
from jax import lax
from jax.experimental import pallas as pl
from jax.experimental.pallas import tpu as pltpu
from jax.sharding import Mesh
from jax.sharding import PartitionSpec as P

BF16 = jnp.bfloat16
F32 = jnp.float32
CAP = 3
HALF = 64
LANES = 128
NT = (((1,), (1,)), ((), ()))
VMEM = pl.BlockSpec(memory_space=pltpu.VMEM)
SMEM = pl.BlockSpec(memory_space=pltpu.SMEM)


def call(body, outs, ins, scratch=()):
    return pl.pallas_call(
        body,
        out_shape=outs,
        in_specs=ins,
        out_specs=jax.tree.map(lambda _: VMEM, outs),
        scratch_shapes=list(scratch),
        compiler_params=pltpu.CompilerParams(vmem_limit_bytes=40 * 1024 * 1024),
    )


def struct(*shape, dtype=BF16):
    return jax.ShapeDtypeStruct(shape, dtype)


def iota(shape, dim):
    return lax.broadcasted_iota(jnp.int32, shape, dim)


def weave(first, second):
    low = iota(first.shape, 1) < HALF
    return (
        jnp.where(low, first, pltpu.roll(second, HALF, 1)),
        jnp.where(low, pltpu.roll(first, HALF, 1), second),
    )


def relative(place_ref, x):
    parity, core = place_ref[0], place_ref[1]
    near = jnp.where(parity == 0, x[:, :LANES], x[:, LANES:])
    far = jnp.where(parity == 0, x[:, LANES:], x[:, :LANES])
    return [jnp.where(core == 0, y, pltpu.roll(y, HALF, 1)) for y in (near, far)]


def pick_body(picked_ref, counts_ref, weights_ref, tokens_ref, grads_ref, out_ref, wide_in, wide_out, rows):
    wide_in[...] = tokens_ref[...].astype(F32)
    wide_out[...] = grads_ref[...].astype(F32)
    rows[...] = jnp.zeros_like(rows)
    for expert in range(out_ref.shape[0]):
        for c in range(CAP):
            token = picked_ref[c, expert]
            scale = jnp.where(c < counts_ref[0, expert], weights_ref[c, expert], 0.0)
            rows[pl.ds(8 * expert + c, 1), :] = wide_out[pl.ds(token, 1), :] * scale
            rows[pl.ds(8 * expert + 4 + c, 1), :] = wide_in[pl.ds(token, 1), :]
    out_ref[...] = rows[...].reshape(out_ref.shape).astype(BF16)


def weight_body(place_ref, down_ref, gate_ref, up_ref, keep_ref, give_ref):
    half = down_ref.shape[1] // 2
    parity = place_ref[0]
    for side, out_ref in ((parity, keep_ref), (1 - parity, give_ref)):
        for k in range(half // LANES):
            columns = pl.ds(pl.multiple_of(side * half + k * LANES, LANES), LANES)
            out_ref[:, k * LANES : (k + 1) * LANES] = down_ref[:, columns]
            one, two = weave(gate_ref[:, columns].astype(F32), up_ref[:, columns].astype(F32))
            start = half + 2 * k * LANES
            out_ref[:, start : start + LANES] = one.astype(BF16)
            out_ref[:, start + LANES : start + 2 * LANES] = two.astype(BF16)


def send_body(blocks_ref, gate_ref, up_ref, out_ref):
    half = gate_ref.shape[1] // 2
    pairs = blocks_ref.shape[0]
    row = iota((8, 2 * LANES), 0)
    for side in range(2):
        for k in range(pairs // 2):
            columns = slice(side * half + k * LANES, side * half + (k + 1) * LANES)
            woven = weave(gate_ref[:, columns].astype(F32), up_ref[:, columns].astype(F32))
            for pair, saved in zip((2 * k, 2 * k + 1), woven):
                early = jnp.concatenate([saved[0:1], saved[1:2]], axis=1)
                late = jnp.concatenate([saved[2:3], saved[2:3]], axis=1)
                block = blocks_ref[pair].astype(F32)
                block = jnp.where(row == 3, early, jnp.where(row == 7, late, block))
                out_ref[2 * pair + side] = block.astype(BF16)


def partial_body(place_ref, rows_ref, own_ref, pair_ref, other_ref, out_ref, saved_ref, keep_ref, give_ref):
    total = rows_ref.shape[0]
    chips = total // 8
    half = own_ref.shape[1]
    row, column = iota((total, total), 0), iota((total, total), 1)
    order = (row % chips == column // 8) & (row // chips == column % 8)
    rows = jnp.dot(order.astype(BF16), rows_ref[...], preferred_element_type=F32)
    slots = CAP * chips
    sent_near, sent_far = relative(place_ref, rows[:slots])
    in_near, _ = relative(place_ref, rows[4 * chips : 4 * chips + slots])
    saved_ref[...] = jnp.concatenate(
        [rows[slots : 4 * chips, :LANES], rows[slots : 4 * chips, LANES:], rows[7 * chips :, :LANES]]
    ).astype(BF16)
    keep, give = weave(sent_near, in_near)
    keep_ref[...] = keep.astype(BF16)
    give_ref[...] = give.astype(BF16)
    sent = jnp.concatenate([sent_near, sent_far], axis=1).astype(BF16)
    down = jnp.concatenate([own_ref[...], other_ref[:HALF], pair_ref[...], other_ref[HALF:]])
    product = jnp.dot(sent, down, preferred_element_type=F32)
    for k in range(half // LANES):
        block = product[:, k * LANES : (k + 1) * LANES]
        one, two = weave(block[: slots // 2], block[slots // 2 :])
        out_ref[2 * k] = one.astype(BF16)
        out_ref[2 * k + 1] = two.astype(BF16)


def hidden_body(parts_ref, saved_ref, out_ref):
    folded = jnp.sum(parts_ref[...].astype(F32), axis=0)
    hidden = jnp.concatenate([folded, pltpu.roll(folded, HALF, 1)])
    hidden = hidden.astype(BF16).astype(F32)
    a = saved_ref[...].astype(F32)
    b = pltpu.roll(a, HALF, 1)
    q = jax.nn.sigmoid(a)
    gate_grad = hidden * b * q * (1.0 + a * (1.0 - q))
    up_grad = hidden * a * q
    activated = a * q * b
    slots = hidden.shape[0]
    out_ref[0, :slots, :] = weave(gate_grad, up_grad)[0].astype(BF16)
    out_ref[0, slots:, :] = weave(activated[: slots // 2], activated[slots // 2 :])[0].astype(BF16)


def slot_body(grads_ref, own_ref, pair_ref, other_ref, out_ref):
    slots = grads_ref.shape[1] * 2 // 3
    chips = out_ref.shape[0]
    half = own_ref.shape[1] // 3
    grads = jnp.concatenate([grads_ref[m, :slots, :] for m in range(grads_ref.shape[0])], axis=1)
    row, slot = iota((8 * chips, slots), 0), iota((8 * chips, slots), 1)
    total = None
    for side, ref, rows in ((0, own_ref, slice(0, HALF)), (1, pair_ref, slice(HALF, LANES))):
        weights = jnp.concatenate([ref[:, half:], other_ref[rows, half:]])
        part = lax.dot_general(grads, weights, NT, preferred_element_type=F32).astype(BF16)
        place = (slot % chips == row // 8) & (row % 8 == 4 * side + slot // chips)
        placed = jnp.dot(place.astype(BF16), part, preferred_element_type=F32)
        total = placed if total is None else total + placed
    out_ref[...] = total.astype(BF16).reshape(out_ref.shape)


def grad_body(place_ref, keep_ref, got_ref, own_ref, pair_ref, other_ref, gate_ref, up_ref, down_ref):
    parity = place_ref[0]
    members = own_ref.shape[0]
    slots = keep_ref.shape[0]
    half = members * HALF
    lefts = [ref[...].astype(F32).T.astype(BF16) for ref in (keep_ref, got_ref)]
    for side, first, second in ((parity, own_ref, other_ref.at[:members]), (1 - parity, pair_ref, other_ref.at[members:])):
        for k in range(members // 2):
            columns = pl.ds(pl.multiple_of(side * half + k * LANES, LANES), LANES)
            both, down = [0.0, 0.0], 0.0
            for left, ref in zip(lefts, (first, second)):
                acts = weave(ref[2 * k, slots:, :].astype(F32), ref[2 * k + 1, slots:, :].astype(F32))
                acts = jnp.concatenate(acts).astype(BF16)
                down = down + jnp.dot(left[:HALF], acts, preferred_element_type=F32)
                for j in range(2):
                    grads = ref[2 * k + j, :slots, :]
                    both[j] = both[j] + jnp.dot(left[HALF:], grads, preferred_element_type=F32)
            gate, up = weave(*both)
            gate_ref[:, columns] = gate
            up_ref[:, columns] = up
            down_ref[:, columns] = down


def token_body(place_ref, index_ref, rows_ref, out_ref):
    tokens = iota((out_ref.shape[0], index_ref.shape[1]), 0)
    for half in range(2):
        owner = (tokens == index_ref[half : half + 1, :]).astype(BF16)
        total = jnp.dot(owner, rows_ref[...], preferred_element_type=F32)
        total = jnp.where(place_ref[1] == 0, total, pltpu.roll(total, HALF, 1))
        out_ref[:, half * LANES : (half + 1) * LANES] = total.astype(BF16)


def swap(x, axis):
    return lax.ppermute(x, axis, [(0, 1), (1, 0)])


def spread(x, axis):
    return lax.all_to_all(x, axis, split_axis=0, concat_axis=0, tiled=True)


def local(pairs, tokens, grad_out, picked, pick_counts, router_weights, saved_gate, saved_up, w_gate, w_up, w_down):
    chips = 2 * pairs
    experts = picked.shape[1]
    token_count, width = tokens.shape
    hidden = w_gate.shape[2]
    slots = CAP * chips
    z = ("m", "p")
    place = jnp.stack([lax.axis_index("p"), lax.axis_index("core")]).astype(jnp.int32)

    outgoing = call(
        pick_body,
        struct(experts, 8, width),
        [SMEM] * 3 + [VMEM] * 2,
        scratch=(
            pltpu.VMEM((token_count, width), F32),
            pltpu.VMEM((token_count, width), F32),
            pltpu.VMEM((8 * experts, width), F32),
        ),
    )(picked[0].T, pick_counts, router_weights[0].T, tokens, grad_out)
    blocks = spread(outgoing, "expert")

    w_keep, w_give = call(weight_body, (struct(HALF, 3 * hidden // 2),) * 2, [SMEM] + [VMEM] * 3)(
        place, w_down[0].T, w_gate[0], w_up[0]
    )
    w_pair = swap(w_give, "p")
    w_other = swap(jnp.concatenate([w_keep, w_pair]), "core")

    rows = call(send_body, struct(chips, 8, width), [VMEM] * 3)(blocks, saved_gate[0], saved_up[0])
    rows = spread(rows, z)
    half = hidden // 2
    parts, saved, keep, give = call(
        partial_body,
        (struct(pairs, slots // 2, LANES),) + (struct(slots, LANES),) * 3,
        [SMEM] + [VMEM] * 4,
    )(place, rows.reshape(8 * chips, width), w_keep[:, :half], w_pair[:, :half], w_other[:, :half])
    got = swap(give, "core")
    parts = spread(parts, "m")
    grads = call(hidden_body, struct(1, 3 * slots // 2, LANES), [VMEM] * 2)(parts, saved)
    grads = lax.all_gather(grads, "m", axis=0, tiled=True)

    back = call(slot_body, struct(chips, 8, LANES), [VMEM] * 4)(grads, w_keep, w_pair, w_other)
    back = spread(back, z)
    back = spread(back.reshape(experts, 16, LANES), "expert")

    lane = jnp.arange(16 * experts, dtype=jnp.int32)
    index = jnp.pad(picked[0], ((0, 0), (0, 1)), constant_values=-1)
    index = jnp.tile(index, (1, 4)).reshape(1, -1)
    far = (lane // 8 % 2) ^ (lane // 4 % 2)
    index = jnp.where(far[None, :] == jnp.arange(2)[:, None], index, -1)
    token_grad = call(token_body, struct(token_count, width), [SMEM] + [VMEM] * 2)(
        place, index, back.reshape(16 * experts, LANES)
    )

    grads_pair = swap(grads, "p")
    grads_other = swap(jnp.concatenate([grads, grads_pair]), "core")
    gate_grad, up_grad, down_grad = call(
        grad_body, (struct(HALF, hidden, dtype=F32),) * 3, [SMEM] + [VMEM] * 5
    )(place, keep, got, grads, grads_pair, grads_other)
    return (token_grad, gate_grad[None], up_grad[None], down_grad.T[None])


def solution(mesh):
    pairs = mesh.shape["dp"] // 4
    fine = Mesh(mesh.devices.reshape(pairs, 2, 2, mesh.shape["expert"]), ("m", "p", "core", "expert"))
    dp = ("m", "p", "core")
    placed = (
        P(dp, "expert"),
        P(dp, "expert"),
        P(dp, None, None),
        P(dp, None),
        P(dp, None, None),
        P("expert", dp, None),
        P("expert", dp, None),
        P("expert", dp, None),
        P("expert", dp, None),
        P("expert", None, dp),
    )
    return jax.shard_map(
        functools.partial(local, pairs),
        mesh=fine,
        in_specs=placed,
        out_specs=(
            P(dp, "expert"),
            P("expert", dp, None),
            P("expert", dp, None),
            P("expert", None, dp),
        ),
        check_vma=False,
    )
```

```python
import functools

import jax
import jax.numpy as jnp
from jax import lax
from jax.experimental import pallas as pl
from jax.experimental.pallas import tpu as pltpu
from jax.sharding import Mesh
from jax.sharding import PartitionSpec as P

BF16 = jnp.bfloat16
F32 = jnp.float32
CAP = 3
HALF = 64
LANES = 128
NT = (((1,), (1,)), ((), ()))
TN = (((0,), (0,)), ((), ()))
VMEM = pl.BlockSpec(memory_space=pltpu.VMEM)
SMEM = pl.BlockSpec(memory_space=pltpu.SMEM)
ANY = pl.BlockSpec(memory_space=pl.ANY)
FETCH = pl.BlockSpec()


def call(body, outs, ins, out_specs=None, scratch=(), limit=40):
    return pl.pallas_call(
        body,
        out_shape=outs,
        in_specs=ins,
        out_specs=jax.tree.map(lambda _: VMEM, outs) if out_specs is None else out_specs,
        scratch_shapes=list(scratch),
        compiler_params=pltpu.CompilerParams(vmem_limit_bytes=limit * 1024 * 1024),
    )


def struct(*shape, dtype=BF16):
    return jax.ShapeDtypeStruct(shape, dtype)


def iota(shape, dim):
    return lax.broadcasted_iota(jnp.int32, shape, dim)


def matmul(left, right, dims=(((1,), (0,)), ((), ()))):
    return lax.dot_general(left, right, dims, preferred_element_type=F32)


def ordered(x, groups):
    total = x.shape[0]
    each = total // groups
    row, column = iota((total, total), 0), iota((total, total), 1)
    order = (row % groups == column // each) & (row // groups == column % each)
    return matmul(order.astype(BF16), x)


def pick_body(picked_ref, counts_ref, weights_ref, tokens_ref, grads_ref, gate_ref, up_ref, out_ref, saved_ref, rows):
    blank = jnp.zeros((4 - CAP, LANES), F32)
    for k in range(saved_ref.shape[0]):
        columns = slice(k * LANES, (k + 1) * LANES)
        parts = [gate_ref[:, columns].astype(F32), blank, up_ref[:, columns].astype(F32), blank]
        saved_ref[k] = jnp.concatenate(parts).astype(BF16)
    experts = out_ref.shape[0]
    diagonal = iota((experts, experts), 0) == iota((experts, experts), 1)
    rows[...] = jnp.zeros_like(rows)
    for c in range(CAP):
        chosen = (iota((tokens_ref.shape[0], experts), 0) == picked_ref[c]).astype(BF16)
        scale = jnp.where(c < counts_ref[...], weights_ref[c], 0.0)
        scale = jnp.sum(jnp.where(diagonal, scale, 0.0), axis=1, keepdims=True)
        sent = matmul(chosen, grads_ref[...], TN) * scale
        taken = matmul(chosen, tokens_ref[...], TN)
        for row, value in ((c, sent), (4 + c, taken)):
            for j in range(rows.shape[0]):
                rows[j, pl.ds(row, experts, stride=8), :] = value[:, j * LANES : (j + 1) * LANES]
    for j in range(rows.shape[0]):
        out_ref[:, :, j * LANES : (j + 1) * LANES] = rows[j].reshape(experts, 8, LANES).astype(BF16)


def send_body(blocks_ref, saved_ref, out_ref):
    for j in range(2):
        out_ref[:, 8 * j : 8 * j + 8, :] = blocks_ref[:, :, j * LANES : (j + 1) * LANES]
    out_ref[:, 16:, :] = saved_ref[...]


def partial_body(place_ref, rows_ref, own_ref, pair_ref, core_ref, out_ref, saved_ref, inner_ref, outer_ref):
    parity, core = place_ref[0], place_ref[1]
    pairs = out_ref.shape[0]
    slots = CAP * pairs
    rows = ordered(rows_ref[...], pairs)
    piece = lambda k: rows[k * pairs : k * pairs + slots]
    saved_ref[0] = piece(16).astype(BF16)
    saved_ref[1] = piece(20).astype(BF16)
    low = iota((slots, LANES), 1) < HALF
    turn = lambda x: jnp.where(core == 0, x, pltpu.roll(x, HALF, 1))
    product = 0.0
    for side, mine_ref, out in ((0, own_ref, inner_ref), (1, pair_ref, outer_ref)):
        here = parity == side
        sent = turn(jnp.where(here, piece(0), piece(8)))
        taken = turn(jnp.where(here, piece(4), piece(12)))
        product = product + matmul(sent.astype(BF16), jnp.concatenate([mine_ref[0], core_ref[side, 0]]))
        out[0] = jnp.where(low, sent, pltpu.roll(taken, HALF, 1)).astype(BF16)
        out[1] = jnp.where(low, pltpu.roll(sent, HALF, 1), taken).astype(BF16)
    for k in range(pairs):
        out_ref[k] = product[:, k * LANES : (k + 1) * LANES].astype(BF16)


def hidden_body(parts_ref, saved_ref, out_ref):
    slots = parts_ref.shape[1]
    hidden = jnp.sum(parts_ref[...].astype(F32), axis=0).astype(BF16).astype(F32)
    a, b = saved_ref[0].astype(F32), saved_ref[1].astype(F32)
    q = jax.nn.sigmoid(a)
    out_ref[0, :slots, :] = (hidden * b * q * (1.0 + a * (1.0 - q))).astype(BF16)
    out_ref[0, slots : 2 * slots, :] = (hidden * a * q).astype(BF16)
    out_ref[0, 2 * slots :, :] = (a * q * b).astype(BF16)


def slot_body(grads_ref, outer_ref, own_ref, pair_ref, core_ref, out_ref, packed_ref):
    pairs = grads_ref.shape[0]
    packed_ref[: -2 * CAP * pairs, :] = grads_ref[...].reshape(-1, LANES)
    packed_ref[-2 * CAP * pairs :, :] = outer_ref[...].reshape(-1, LANES)
    slots = CAP * pairs
    total = [0.0, 0.0]
    for kind in range(2):
        grads = jnp.concatenate(
            [grads_ref[m, kind * slots : (kind + 1) * slots, :] for m in range(pairs)], axis=1
        )
        for side, mine_ref in enumerate((own_ref, pair_ref)):
            weights = jnp.concatenate([mine_ref[1 + kind], core_ref[side, 1 + kind]])
            total[side] = total[side] + matmul(grads, weights, NT)
    row, slot = iota((8 * pairs, slots), 0), iota((8 * pairs, slots), 1)
    placed = 0.0
    for half in range(2):
        place = (slot % pairs == row // 8) & (row % 8 == 4 * half + slot // pairs)
        placed = placed + matmul(place.astype(BF16), total[half].astype(BF16))
    out_ref[...] = placed.astype(BF16).reshape(out_ref.shape)


def join_body(_, own_ref, inner_ref, pair_ref, out_ref):
    slots = inner_ref.shape[1]
    split = own_ref.shape[0] - 2 * slots
    out_ref[0, :split, :] = own_ref[:split, :]
    out_ref[0, split:, :] = inner_ref[1]
    out_ref[1, :split, :] = pair_ref[:split, :]
    out_ref[1, split:, :] = pair_ref[split + slots :, :]


def grad_body(inner_ref, own_ref, pair_ref, core_ref, gate_ref, up_ref, down_ref, done_ref):
    slots = inner_ref.shape[1]
    split = own_ref.shape[0] - 2 * slots
    lefts = [inner_ref[0], pair_ref[split : split + slots, :], core_ref[0, split:, :], core_ref[1, split:, :]]
    left = jnp.concatenate(lefts).astype(F32).T.astype(BF16)
    sent, taken = left[:HALF], left[HALF:]
    rights = (own_ref, pair_ref, core_ref.at[0], core_ref.at[1])
    for m in range(split // (3 * slots)):
        columns = slice(m * LANES, (m + 1) * LANES)
        for kind, (rows, out_ref) in enumerate(((taken, gate_ref), (taken, up_ref), (sent, down_ref))):
            start = (3 * m + kind) * slots
            right = jnp.concatenate([ref[start : start + slots, :] for ref in rights])
            out_ref[:, columns] = matmul(rows, right)
    done_ref[...] = jnp.zeros_like(done_ref)


def token_body(place_ref, _, index_ref, rows_ref, out_ref):
    parity, core = place_ref[0], place_ref[1]
    tokens = iota((out_ref.shape[0], index_ref.shape[1]), 0)
    sides = []
    for side in range(2):
        owner = (tokens == index_ref[side : side + 1, :]).astype(BF16)
        total = matmul(owner, rows_ref[...])
        sides.append(jnp.where(core == 0, total, pltpu.roll(total, HALF, 1)))
    near, far = sides
    out_ref[:, :LANES] = jnp.where(parity == 0, near, far).astype(BF16)
    out_ref[:, LANES:] = jnp.where(parity == 0, far, near).astype(BF16)


def swap(x, axis):
    return lax.ppermute(x, axis, [(0, 1), (1, 0)])


def spread(x, axis):
    return lax.all_to_all(x, axis, split_axis=0, concat_axis=0, tiled=True)


def local(pairs, tokens, grad_out, picked, pick_counts, router_weights, saved_gate, saved_up, w_gate, w_up, w_down):
    experts = picked.shape[1]
    token_count, width = tokens.shape
    hidden = w_gate.shape[2]
    slots = CAP * pairs
    place = jnp.stack([lax.axis_index("p"), lax.axis_index("core")]).astype(jnp.int32)

    outgoing, saved = call(
        pick_body,
        (struct(experts, 8, width), struct(pairs, 8, LANES)),
        [FETCH] * 7,
        scratch=(pltpu.VMEM((width // LANES, 8 * experts, LANES), F32),),
        limit=60,
    )(picked.transpose(2, 0, 1), pick_counts, router_weights.transpose(2, 0, 1), tokens, grad_out, saved_gate[0], saved_up[0])
    blocks = spread(outgoing, "expert")

    own = jnp.stack([w_down[0].T, w_gate[0], w_up[0]])
    pair = swap(own, "p")

    rows = call(send_body, struct(pairs, 24, LANES), [VMEM] * 2)(blocks, saved)
    core = swap(jnp.stack([own, pair]) + rows[0, 0, 0] * 0, "core")
    rows = spread(rows, "m")
    parts, saved, inner, outer = call(
        partial_body,
        (struct(pairs, slots, LANES),) + (struct(2, slots, LANES),) * 3,
        [SMEM] + [VMEM] * 4,
    )(place, rows.reshape(24 * pairs, LANES), own, pair, core)

    parts = spread(parts, "m")
    grads = call(hidden_body, struct(1, 3 * slots, LANES), [VMEM] * 2)(parts, saved)
    grads = lax.all_gather(grads, "m", axis=0, tiled=True)
    packed_rows = 3 * slots * pairs + 2 * slots
    back, packed = call(
        slot_body, (struct(pairs, 8, LANES), struct(packed_rows, LANES)), [VMEM] * 5
    )(grads, outer, own, pair, core)
    packed_pair = swap(packed, "p")
    back = spread(back, "m")
    packed_core = call(join_body, struct(2, packed_rows - slots, LANES), [ANY] + [VMEM] * 3)(
        back, packed, inner, packed_pair
    )
    packed_core = swap(packed_core, "core")
    back = spread(back, "expert")

    gate_grad, up_grad, down_grad, done = call(
        grad_body, (struct(HALF, hidden, dtype=F32),) * 3 + (struct(8, LANES, dtype=F32),), [VMEM] * 4
    )(inner, packed, packed_pair, packed_core)

    index = jnp.pad(picked[0], ((0, 0), (0, 1)), constant_values=-1)
    index = jnp.tile(index, (1, 2)).reshape(1, -1)
    upper = jnp.arange(8 * experts, dtype=jnp.int32)[None, :] // 4 % 2
    index = jnp.where(upper == jnp.arange(2)[:, None], index, -1)
    token_grad = call(token_body, struct(token_count, width), [SMEM] + [VMEM] * 3)(
        place, done, index, back.reshape(8 * experts, LANES)
    )
    return (token_grad, gate_grad[None], up_grad[None], down_grad.T[None])


def solution(mesh):
    pairs = mesh.shape["dp"] // 4
    fine = Mesh(mesh.devices.reshape(pairs, 2, 2, mesh.shape["expert"]), ("m", "p", "core", "expert"))
    dp = ("m", "p", "core")
    placed = (
        P(dp, "expert"),
        P(dp, "expert"),
        P(dp, None, None),
        P(dp, None),
        P(dp, None, None),
        P("expert", dp, None),
        P("expert", dp, None),
        P("expert", dp, None),
        P("expert", dp, None),
        P("expert", None, dp),
    )
    return jax.shard_map(
        functools.partial(local, pairs),
        mesh=fine,
        in_specs=placed,
        out_specs=(
            P(dp, "expert"),
            P("expert", dp, None),
            P("expert", dp, None),
            P("expert", None, dp),
        ),
        check_vma=False,
    )
```

```python
import functools

import jax
import jax.numpy as jnp
from jax import lax
from jax.experimental import pallas as pl
from jax.experimental.pallas import tpu as pltpu
from jax.sharding import Mesh
from jax.sharding import PartitionSpec as P

BF16 = jnp.bfloat16
F32 = jnp.float32
CAP = 3
HALF = 64
LANES = 128
NT = (((1,), (1,)), ((), ()))
TN = (((0,), (0,)), ((), ()))
VMEM = pl.BlockSpec(memory_space=pltpu.VMEM)
SMEM = pl.BlockSpec(memory_space=pltpu.SMEM)
ANY = pl.BlockSpec(memory_space=pl.ANY)
FETCH = pl.BlockSpec()


def call(body, outs, ins, out_specs=None, scratch=(), limit=24):
    return pl.pallas_call(
        body,
        out_shape=outs,
        in_specs=ins,
        out_specs=jax.tree.map(lambda _: VMEM, outs) if out_specs is None else out_specs,
        scratch_shapes=list(scratch),
        compiler_params=pltpu.CompilerParams(vmem_limit_bytes=limit * 1024 * 1024),
    )


def struct(*shape, dtype=BF16):
    return jax.ShapeDtypeStruct(shape, dtype)


def iota(shape, dim):
    return lax.broadcasted_iota(jnp.int32, shape, dim)


def matmul(left, right, dims=(((1,), (0,)), ((), ()))):
    return lax.dot_general(left, right, dims, preferred_element_type=F32)


def ordered(x, groups):
    total = x.shape[0]
    each = total // groups
    row, column = iota((total, total), 0), iota((total, total), 1)
    order = (row % groups == column // each) & (row // groups == column % each)
    return matmul(order.astype(BF16), x)


def pick_body(picked_ref, counts_ref, weights_ref, tokens_ref, grads_ref, gate_ref, up_ref, out_ref, saved_ref, rows):
    blank = jnp.zeros((4 - CAP, LANES), F32)
    for k in range(saved_ref.shape[0]):
        columns = slice(k * LANES, (k + 1) * LANES)
        parts = [gate_ref[:, columns].astype(F32), blank, up_ref[:, columns].astype(F32), blank]
        saved_ref[k] = jnp.concatenate(parts).astype(BF16)
    experts = out_ref.shape[0]
    diagonal = iota((experts, experts), 0) == iota((experts, experts), 1)
    rows[...] = jnp.zeros_like(rows)
    for c in range(CAP):
        chosen = (iota((tokens_ref.shape[0], experts), 0) == picked_ref[c]).astype(BF16)
        scale = jnp.where(c < counts_ref[...], weights_ref[c], 0.0)
        scale = jnp.sum(jnp.where(diagonal, scale, 0.0), axis=1, keepdims=True)
        sent = matmul(chosen, grads_ref[...], TN) * scale
        taken = matmul(chosen, tokens_ref[...], TN)
        for row, value in ((c, sent), (4 + c, taken)):
            for j in range(rows.shape[0]):
                rows[j, pl.ds(row, experts, stride=8), :] = value[:, j * LANES : (j + 1) * LANES]
    for j in range(rows.shape[0]):
        out_ref[:, :, j * LANES : (j + 1) * LANES] = rows[j].reshape(experts, 8, LANES).astype(BF16)


def send_body(blocks_ref, saved_ref, out_ref):
    for j in range(2):
        out_ref[:, 8 * j : 8 * j + 8, :] = blocks_ref[:, :, j * LANES : (j + 1) * LANES]
    out_ref[:, 16:, :] = saved_ref[...]


def partial_body(place_ref, rows_ref, own_ref, pair_ref, core_ref, out_ref, saved_ref, inner_ref, outer_ref):
    parity, core = place_ref[0], place_ref[1]
    pairs = out_ref.shape[0]
    slots = CAP * pairs
    rows = ordered(rows_ref[...], pairs)
    piece = lambda k: rows[k * pairs : k * pairs + slots]
    saved_ref[0] = piece(16).astype(BF16)
    saved_ref[1] = piece(20).astype(BF16)
    low = iota((slots, LANES), 1) < HALF
    turn = lambda x: jnp.where(core == 0, x, pltpu.roll(x, HALF, 1))
    product = 0.0
    for side, mine_ref, out in ((0, own_ref, inner_ref), (1, pair_ref, outer_ref)):
        here = parity == side
        sent = turn(jnp.where(here, piece(0), piece(8)))
        taken = turn(jnp.where(here, piece(4), piece(12)))
        product = product + matmul(sent.astype(BF16), jnp.concatenate([mine_ref[...], core_ref[side]]))
        out[0] = jnp.where(low, sent, pltpu.roll(taken, HALF, 1)).astype(BF16)
        out[1] = jnp.where(low, pltpu.roll(sent, HALF, 1), taken).astype(BF16)
    for k in range(pairs):
        out_ref[k] = product[:, k * LANES : (k + 1) * LANES].astype(BF16)


def hidden_body(parts_ref, saved_ref, out_ref):
    slots = parts_ref.shape[1]
    hidden = jnp.sum(parts_ref[...].astype(F32), axis=0).astype(BF16).astype(F32)
    a, b = saved_ref[0].astype(F32), saved_ref[1].astype(F32)
    q = jax.nn.sigmoid(a)
    out_ref[0, :slots, :] = (hidden * b * q * (1.0 + a * (1.0 - q))).astype(BF16)
    out_ref[0, slots : 2 * slots, :] = (hidden * a * q).astype(BF16)
    out_ref[0, 2 * slots :, :] = (a * q * b).astype(BF16)


def slot_body(grads_ref, outer_ref, own_ref, pair_ref, core_ref, out_ref, packed_ref):
    pairs = grads_ref.shape[0]
    packed_ref[: -2 * CAP * pairs, :] = grads_ref[...].reshape(-1, LANES)
    packed_ref[-2 * CAP * pairs :, :] = outer_ref[...].reshape(-1, LANES)
    slots = CAP * pairs
    total = [0.0, 0.0]
    for kind in range(2):
        grads = jnp.concatenate(
            [grads_ref[m, kind * slots : (kind + 1) * slots, :] for m in range(pairs)], axis=1
        )
        for side, mine_ref in enumerate((own_ref, pair_ref)):
            weights = jnp.concatenate([mine_ref[kind], core_ref[side, kind]])
            total[side] = total[side] + matmul(grads, weights, NT)
    row, slot = iota((8 * pairs, slots), 0), iota((8 * pairs, slots), 1)
    placed = 0.0
    for half in range(2):
        place = (slot % pairs == row // 8) & (row % 8 == 4 * half + slot // pairs)
        placed = placed + matmul(place.astype(BF16), total[half].astype(BF16))
    out_ref[...] = placed.astype(BF16).reshape(out_ref.shape)


def join_body(_, own_ref, inner_ref, pair_ref, out_ref):
    slots = inner_ref.shape[1]
    split = own_ref.shape[0]
    out_ref[0, :split, :] = own_ref[...]
    out_ref[0, split:, :] = inner_ref[1]
    out_ref[1, :split, :] = pair_ref[:split, :]
    out_ref[1, split:, :] = pair_ref[split + slots :, :]


def grad_body(inner_ref, own_ref, pair_ref, core_ref, gate_ref, up_ref, down_ref, done_ref):
    slots = inner_ref.shape[1]
    split = own_ref.shape[0]
    lefts = [inner_ref[0], pair_ref[split : split + slots, :], core_ref[0, split:, :], core_ref[1, split:, :]]
    left = jnp.concatenate(lefts).astype(F32).T.astype(BF16)
    sent, taken = left[:HALF], left[HALF:]
    rights = (own_ref, pair_ref, core_ref.at[0], core_ref.at[1])
    for m in range(split // (3 * slots)):
        columns = slice(m * LANES, (m + 1) * LANES)
        for kind, (rows, out_ref) in enumerate(((taken, gate_ref), (taken, up_ref), (sent, down_ref))):
            start = (3 * m + kind) * slots
            right = jnp.concatenate([ref[start : start + slots, :] for ref in rights])
            out_ref[:, columns] = matmul(rows, right)
    done_ref[...] = jnp.zeros_like(done_ref)


def token_body(place_ref, _, index_ref, rows_ref, out_ref):
    parity, core = place_ref[0], place_ref[1]
    tokens = iota((out_ref.shape[0], index_ref.shape[1]), 0)
    sides = []
    for side in range(2):
        owner = (tokens == index_ref[side : side + 1, :]).astype(BF16)
        total = matmul(owner, rows_ref[...])
        sides.append(jnp.where(core == 0, total, pltpu.roll(total, HALF, 1)))
    near, far = sides
    out_ref[:, :LANES] = jnp.where(parity == 0, near, far).astype(BF16)
    out_ref[:, LANES:] = jnp.where(parity == 0, far, near).astype(BF16)


def swap(x, axis):
    return lax.ppermute(x, axis, [(0, 1), (1, 0)])


def spread(x, axis):
    return lax.all_to_all(x, axis, split_axis=0, concat_axis=0, tiled=True)


def local(pairs, tokens, grad_out, picked, pick_counts, router_weights, saved_gate, saved_up, w_gate, w_up, w_down):
    experts = picked.shape[1]
    token_count, width = tokens.shape
    hidden = w_gate.shape[2]
    slots = CAP * pairs
    place = jnp.stack([lax.axis_index("p"), lax.axis_index("core")]).astype(jnp.int32)

    outgoing, saved = call(
        pick_body,
        (struct(experts, 8, width), struct(pairs, 8, LANES)),
        [FETCH] * 7,
        scratch=(pltpu.VMEM((width // LANES, 8 * experts, LANES), F32),),
        limit=60,
    )(picked.transpose(2, 0, 1), pick_counts, router_weights.transpose(2, 0, 1), tokens, grad_out, saved_gate[0], saved_up[0])
    blocks = spread(outgoing, "expert")

    down = w_down[0].T
    down_pair = swap(down, "p")
    down_core = swap(jnp.stack([down, down_pair]), "core")
    own = jnp.stack([w_gate[0], w_up[0]])
    pair = swap(own, "p")
    core = swap(jnp.stack([own, pair]), "core")

    rows = call(send_body, struct(pairs, 24, LANES), [VMEM] * 2)(blocks, saved)
    rows = spread(rows, "m")
    parts, saved, inner, outer = call(
        partial_body,
        (struct(pairs, slots, LANES),) + (struct(2, slots, LANES),) * 3,
        [SMEM] + [VMEM] * 4,
    )(place, rows.reshape(24 * pairs, LANES), down, down_pair, down_core)

    parts = spread(parts, "m")
    grads = call(hidden_body, struct(1, 3 * slots, LANES), [VMEM] * 2)(parts, saved)
    grads = lax.all_gather(grads, "m", axis=0, tiled=True)
    flat = grads.reshape(3 * slots * pairs, LANES)
    packed_rows = 3 * slots * pairs + 2 * slots
    back, packed = call(
        slot_body, (struct(pairs, 8, LANES), struct(packed_rows, LANES)), [VMEM] * 5
    )(grads, outer, own, pair, core)
    packed_pair = swap(packed, "p")
    back = spread(back, "m")
    packed_core = call(join_body, struct(2, packed_rows - slots, LANES), [ANY] + [VMEM] * 3)(
        back, flat, inner, packed_pair
    )
    packed_core = swap(packed_core, "core")
    back = spread(back, "expert")

    gate_grad, up_grad, down_grad, done = call(
        grad_body, (struct(HALF, hidden, dtype=F32),) * 3 + (struct(8, LANES, dtype=F32),), [VMEM] * 4
    )(inner, flat, packed_pair, packed_core)

    index = jnp.pad(picked[0], ((0, 0), (0, 1)), constant_values=-1)
    index = jnp.tile(index, (1, 2)).reshape(1, -1)
    upper = jnp.arange(8 * experts, dtype=jnp.int32)[None, :] // 4 % 2
    index = jnp.where(upper == jnp.arange(2)[:, None], index, -1)
    token_grad = call(token_body, struct(token_count, width), [SMEM] + [VMEM] * 3)(
        place, done, index, back.reshape(8 * experts, LANES)
    )
    return (token_grad, gate_grad[None], up_grad[None], down_grad.T[None])


def solution(mesh):
    pairs = mesh.shape["dp"] // 4
    fine = Mesh(mesh.devices.reshape(pairs, 2, 2, mesh.shape["expert"]), ("m", "p", "core", "expert"))
    dp = ("m", "p", "core")
    placed = (
        P(dp, "expert"),
        P(dp, "expert"),
        P(dp, None, None),
        P(dp, None),
        P(dp, None, None),
        P("expert", dp, None),
        P("expert", dp, None),
        P("expert", dp, None),
        P("expert", dp, None),
        P("expert", None, dp),
    )
    return jax.shard_map(
        functools.partial(local, pairs),
        mesh=fine,
        in_specs=placed,
        out_specs=(
            P(dp, "expert"),
            P("expert", dp, None),
            P("expert", dp, None),
            P("expert", None, dp),
        ),
        check_vma=False,
    )
```

```python
import functools

import jax
import jax.numpy as jnp
from jax import lax
from jax.experimental import pallas as pl
from jax.experimental.pallas import tpu as pltpu
from jax.sharding import Mesh
from jax.sharding import PartitionSpec as P

BF16 = jnp.bfloat16
F32 = jnp.float32
CAP = 3
HALF = 64
LANES = 128
NT = (((1,), (1,)), ((), ()))
TN = (((0,), (0,)), ((), ()))
VMEM = pl.BlockSpec(memory_space=pltpu.VMEM)
SMEM = pl.BlockSpec(memory_space=pltpu.SMEM)
ANY = pl.BlockSpec(memory_space=pl.ANY)
FETCH = pl.BlockSpec()


def call(body, outs, ins, out_specs=None, scratch=(), limit=24):
    return pl.pallas_call(
        body,
        out_shape=outs,
        in_specs=ins,
        out_specs=jax.tree.map(lambda _: VMEM, outs) if out_specs is None else out_specs,
        scratch_shapes=list(scratch),
        compiler_params=pltpu.CompilerParams(vmem_limit_bytes=limit * 1024 * 1024),
    )


def struct(*shape, dtype=BF16):
    return jax.ShapeDtypeStruct(shape, dtype)


def iota(shape, dim):
    return lax.broadcasted_iota(jnp.int32, shape, dim)


def matmul(left, right, dims=(((1,), (0,)), ((), ()))):
    return lax.dot_general(left, right, dims, preferred_element_type=F32)


def ordered(x, groups):
    total = x.shape[0]
    each = total // groups
    row, column = iota((total, total), 0), iota((total, total), 1)
    order = (row % groups == column // each) & (row // groups == column % each)
    return matmul(order.astype(BF16), x)


def pick_body(picked_ref, counts_ref, weights_ref, tokens_ref, grads_ref, gate_ref, up_ref, out_ref, saved_ref, rows):
    blank = jnp.zeros((4 - CAP, LANES), F32)
    for k in range(saved_ref.shape[0]):
        columns = slice(k * LANES, (k + 1) * LANES)
        parts = [gate_ref[:, columns].astype(F32), blank, up_ref[:, columns].astype(F32), blank]
        saved_ref[k] = jnp.concatenate(parts).astype(BF16)
    experts = out_ref.shape[0]
    diagonal = iota((experts, experts), 0) == iota((experts, experts), 1)
    rows[...] = jnp.zeros_like(rows)
    for c in range(CAP):
        chosen = (iota((tokens_ref.shape[0], experts), 0) == picked_ref[c]).astype(BF16)
        scale = jnp.where(c < counts_ref[...], weights_ref[c], 0.0)
        scale = jnp.sum(jnp.where(diagonal, scale, 0.0), axis=1, keepdims=True)
        sent = matmul(chosen, grads_ref[...], TN) * scale
        taken = matmul(chosen, tokens_ref[...], TN)
        for row, value in ((c, sent), (4 + c, taken)):
            for j in range(rows.shape[0]):
                rows[j, pl.ds(row, experts, stride=8), :] = value[:, j * LANES : (j + 1) * LANES]
    for j in range(rows.shape[0]):
        out_ref[:, :, j * LANES : (j + 1) * LANES] = rows[j].reshape(experts, 8, LANES).astype(BF16)


def send_body(blocks_ref, saved_ref, out_ref):
    for j in range(2):
        out_ref[:, 8 * j : 8 * j + 8, :] = blocks_ref[:, :, j * LANES : (j + 1) * LANES]
    out_ref[:, 16:, :] = saved_ref[...]


def partial_body(place_ref, rows_ref, own_ref, pair_ref, core_ref, out_ref, saved_ref, inner_ref, outer_ref):
    parity, core = place_ref[0], place_ref[1]
    pairs = out_ref.shape[0]
    slots = CAP * pairs
    rows = ordered(rows_ref[...], pairs)
    piece = lambda k: rows[k * pairs : k * pairs + slots]
    saved_ref[0] = piece(16).astype(BF16)
    saved_ref[1] = piece(20).astype(BF16)
    low = iota((slots, LANES), 1) < HALF
    turn = lambda x: jnp.where(core == 0, x, pltpu.roll(x, HALF, 1))
    product = 0.0
    for side, mine_ref, out in ((0, own_ref, inner_ref), (1, pair_ref, outer_ref)):
        here = parity == side
        sent = turn(jnp.where(here, piece(0), piece(8)))
        taken = turn(jnp.where(here, piece(4), piece(12)))
        product = product + matmul(sent.astype(BF16), jnp.concatenate([mine_ref[...], core_ref[side]]))
        out[0] = jnp.where(low, sent, pltpu.roll(taken, HALF, 1)).astype(BF16)
        out[1] = jnp.where(low, pltpu.roll(sent, HALF, 1), taken).astype(BF16)
    for k in range(pairs):
        out_ref[k] = product[:, k * LANES : (k + 1) * LANES].astype(BF16)


def hidden_body(parts_ref, saved_ref, out_ref):
    slots = parts_ref.shape[1]
    hidden = jnp.sum(parts_ref[...].astype(F32), axis=0).astype(BF16).astype(F32)
    a, b = saved_ref[0].astype(F32), saved_ref[1].astype(F32)
    q = jax.nn.sigmoid(a)
    out_ref[0, :slots, :] = (hidden * b * q * (1.0 + a * (1.0 - q))).astype(BF16)
    out_ref[0, slots : 2 * slots, :] = (hidden * a * q).astype(BF16)
    out_ref[0, 2 * slots :, :] = (a * q * b).astype(BF16)


def slot_body(grads_ref, outer_ref, own_ref, pair_ref, core_ref, out_ref, packed_ref):
    pairs = grads_ref.shape[0]
    packed_ref[: -2 * CAP * pairs, :] = grads_ref[...].reshape(-1, LANES)
    packed_ref[-2 * CAP * pairs :, :] = outer_ref[...].reshape(-1, LANES)
    slots = CAP * pairs
    total = [0.0, 0.0]
    for kind in range(2):
        grads = jnp.concatenate(
            [grads_ref[m, kind * slots : (kind + 1) * slots, :] for m in range(pairs)], axis=1
        )
        for side, mine_ref in enumerate((own_ref, pair_ref)):
            weights = jnp.concatenate([mine_ref[kind], core_ref[side, kind]])
            total[side] = total[side] + matmul(grads, weights, NT)
    row, slot = iota((8 * pairs, slots), 0), iota((8 * pairs, slots), 1)
    placed = 0.0
    for half in range(2):
        place = (slot % pairs == row // 8) & (row % 8 == 4 * half + slot // pairs)
        placed = placed + matmul(place.astype(BF16), total[half].astype(BF16))
    out_ref[...] = placed.astype(BF16).reshape(out_ref.shape)


def join_body(_, own_ref, inner_ref, pair_ref, out_ref):
    slots = inner_ref.shape[1]
    split = own_ref.shape[0]
    out_ref[0, :split, :] = own_ref[...]
    out_ref[0, split:, :] = inner_ref[1]
    out_ref[1, :split, :] = pair_ref[:split, :]
    out_ref[1, split:, :] = pair_ref[split + slots :, :]


def grad_body(inner_ref, own_ref, pair_ref, core_ref, gate_ref, up_ref, down_ref, done_ref):
    slots = inner_ref.shape[1]
    split = own_ref.shape[0]
    lefts = [inner_ref[0], pair_ref[split : split + slots, :], core_ref[0, split:, :], core_ref[1, split:, :]]
    left = jnp.concatenate(lefts).astype(F32).T.astype(BF16)
    sent, taken = left[:HALF], left[HALF:]
    rights = (own_ref, pair_ref, core_ref.at[0], core_ref.at[1])
    for m in range(split // (3 * slots)):
        columns = slice(m * LANES, (m + 1) * LANES)
        for kind, (rows, out_ref) in enumerate(((taken, gate_ref), (taken, up_ref), (sent, down_ref))):
            start = (3 * m + kind) * slots
            right = jnp.concatenate([ref[start : start + slots, :] for ref in rights])
            out_ref[:, columns] = matmul(rows, right)
    done_ref[...] = jnp.zeros_like(done_ref)


def token_body(place_ref, _, index_ref, rows_ref, out_ref):
    parity, core = place_ref[0], place_ref[1]
    tokens = iota((out_ref.shape[0], index_ref.shape[1]), 0)
    sides = []
    for side in range(2):
        owner = (tokens == index_ref[side : side + 1, :]).astype(BF16)
        total = matmul(owner, rows_ref[...])
        sides.append(jnp.where(core == 0, total, pltpu.roll(total, HALF, 1)))
    near, far = sides
    out_ref[:, :LANES] = jnp.where(parity == 0, near, far).astype(BF16)
    out_ref[:, LANES:] = jnp.where(parity == 0, far, near).astype(BF16)


def swap(x, axis):
    return lax.ppermute(x, axis, [(0, 1), (1, 0)])


def transpose(x, pairs):
    moves = [(m * pairs + f, f * pairs + m) for m in range(pairs) for f in range(pairs)]
    return lax.ppermute(x, ("m", "expert"), moves)


def spread(x, axis):
    return lax.all_to_all(x, axis, split_axis=0, concat_axis=0, tiled=True)


def local(pairs, tokens, grad_out, picked, pick_counts, router_weights, saved_gate, saved_up, w_gate, w_up, w_down):
    experts = picked.shape[1]
    token_count, width = tokens.shape
    hidden = w_gate.shape[2]
    slots = CAP * pairs
    place = jnp.stack([lax.axis_index("p"), lax.axis_index("core")]).astype(jnp.int32)

    outgoing, saved = call(
        pick_body,
        (struct(experts, 8, width), struct(pairs, 8, LANES)),
        [FETCH] * 7,
        scratch=(pltpu.VMEM((width // LANES, 8 * experts, LANES), F32),),
        limit=60,
    )(picked.transpose(2, 0, 1), pick_counts, router_weights.transpose(2, 0, 1), tokens, grad_out, saved_gate[0], saved_up[0])
    blocks = spread(outgoing, "expert")

    down = w_down[0].T
    down_pair = swap(down, "p")
    down_core = swap(jnp.stack([down, down_pair]), "core")
    own = jnp.stack([w_gate[0], w_up[0]])
    pair = swap(own, "p")
    core = swap(jnp.stack([own, pair]), "core")

    rows = call(send_body, struct(pairs, 24, LANES), [VMEM] * 2)(blocks, saved)
    rows = spread(rows, "m")
    parts, saved, inner, outer = call(
        partial_body,
        (struct(pairs, slots, LANES),) + (struct(2, slots, LANES),) * 3,
        [SMEM] + [VMEM] * 4,
    )(place, rows.reshape(24 * pairs, LANES), down, down_pair, down_core)

    parts = spread(parts, "m")
    grads = call(hidden_body, struct(1, 3 * slots, LANES), [VMEM] * 2)(parts, saved)
    grads = lax.all_gather(grads, "m", axis=0, tiled=True)
    flat = grads.reshape(3 * slots * pairs, LANES)
    packed_rows = 3 * slots * pairs + 2 * slots
    back, packed = call(
        slot_body, (struct(pairs, 8, LANES), struct(packed_rows, LANES)), [VMEM] * 5
    )(grads, outer, own, pair, core)
    packed_pair = swap(packed, "p")
    back = spread(back, "expert")
    packed_core = call(join_body, struct(2, packed_rows - slots, LANES), [ANY] + [VMEM] * 3)(
        back, flat, inner, packed_pair
    )
    packed_core = swap(packed_core, "core")
    back = transpose(back, pairs)

    gate_grad, up_grad, down_grad, done = call(
        grad_body, (struct(HALF, hidden, dtype=F32),) * 3 + (struct(8, LANES, dtype=F32),), [VMEM] * 4
    )(inner, flat, packed_pair, packed_core)

    index = jnp.pad(picked[0], ((0, 0), (0, 1)), constant_values=-1)
    index = jnp.tile(index, (1, 2)).reshape(1, -1)
    upper = jnp.arange(8 * experts, dtype=jnp.int32)[None, :] // 4 % 2
    index = jnp.where(upper == jnp.arange(2)[:, None], index, -1)
    token_grad = call(token_body, struct(token_count, width), [SMEM] + [VMEM] * 3)(
        place, done, index, back.reshape(8 * experts, LANES)
    )
    return (token_grad, gate_grad[None], up_grad[None], down_grad.T[None])


def solution(mesh):
    pairs = mesh.shape["dp"] // 4
    fine = Mesh(mesh.devices.reshape(pairs, 2, 2, mesh.shape["expert"]), ("m", "p", "core", "expert"))
    dp = ("m", "p", "core")
    placed = (
        P(dp, "expert"),
        P(dp, "expert"),
        P(dp, None, None),
        P(dp, None),
        P(dp, None, None),
        P("expert", dp, None),
        P("expert", dp, None),
        P("expert", dp, None),
        P("expert", dp, None),
        P("expert", None, dp),
    )
    return jax.shard_map(
        functools.partial(local, pairs),
        mesh=fine,
        in_specs=placed,
        out_specs=(
            P(dp, "expert"),
            P("expert", dp, None),
            P("expert", dp, None),
            P("expert", None, dp),
        ),
        check_vma=False,
    )
```

```python
import functools

import jax
import jax.numpy as jnp
from jax import lax
from jax.experimental import pallas as pl
from jax.experimental.pallas import tpu as pltpu
from jax.sharding import Mesh
from jax.sharding import PartitionSpec as P

BF16 = jnp.bfloat16
F32 = jnp.float32
CAP = 3
HALF = 64
LANES = 128
NT = (((1,), (1,)), ((), ()))
TN = (((0,), (0,)), ((), ()))
VMEM = pl.BlockSpec(memory_space=pltpu.VMEM)
SMEM = pl.BlockSpec(memory_space=pltpu.SMEM)
ANY = pl.BlockSpec(memory_space=pl.ANY)
FETCH = pl.BlockSpec()


def call(body, outs, ins, out_specs=None, scratch=(), limit=24):
    return pl.pallas_call(
        body,
        out_shape=outs,
        in_specs=ins,
        out_specs=jax.tree.map(lambda _: VMEM, outs) if out_specs is None else out_specs,
        scratch_shapes=list(scratch),
        compiler_params=pltpu.CompilerParams(vmem_limit_bytes=limit * 1024 * 1024),
    )


def struct(*shape, dtype=BF16):
    return jax.ShapeDtypeStruct(shape, dtype)


def iota(shape, dim):
    return lax.broadcasted_iota(jnp.int32, shape, dim)


def matmul(left, right, dims=(((1,), (0,)), ((), ()))):
    return lax.dot_general(left, right, dims, preferred_element_type=F32)


def ordered(x, groups):
    total = x.shape[0]
    each = total // groups
    row, column = iota((total, total), 0), iota((total, total), 1)
    order = (row % groups == column // each) & (row // groups == column % each)
    return matmul(order.astype(BF16), x)


def saved_body(gate_ref, up_ref, out_ref):
    blank = jnp.zeros((4 - CAP, LANES), F32)
    for k in range(out_ref.shape[0]):
        columns = slice(k * LANES, (k + 1) * LANES)
        parts = [gate_ref[:, columns].astype(F32), blank, up_ref[:, columns].astype(F32), blank]
        out_ref[k] = jnp.concatenate(parts).astype(BF16)


def pick_body(picked_ref, counts_ref, weights_ref, tokens_ref, grads_ref, out_ref, rows):
    experts = out_ref.shape[0]
    diagonal = iota((experts, experts), 0) == iota((experts, experts), 1)
    rows[...] = jnp.zeros_like(rows)
    for c in range(CAP):
        chosen = (iota((tokens_ref.shape[0], experts), 0) == picked_ref[c]).astype(BF16)
        scale = jnp.where(c < counts_ref[...], weights_ref[c], 0.0)
        scale = jnp.sum(jnp.where(diagonal, scale, 0.0), axis=1, keepdims=True)
        sent = matmul(chosen, grads_ref[...], TN) * scale
        taken = matmul(chosen, tokens_ref[...], TN)
        for row, value in ((c, sent), (4 + c, taken)):
            for j in range(rows.shape[0]):
                rows[j, pl.ds(row, experts, stride=8), :] = value[:, j * LANES : (j + 1) * LANES]
    for j in range(rows.shape[0]):
        out_ref[:, :, j * LANES : (j + 1) * LANES] = rows[j].reshape(experts, 8, LANES).astype(BF16)


def send_body(blocks_ref, saved_ref, out_ref):
    for j in range(2):
        out_ref[:, 8 * j : 8 * j + 8, :] = blocks_ref[:, :, j * LANES : (j + 1) * LANES]
    out_ref[:, 16:, :] = saved_ref[...]


def partial_body(place_ref, rows_ref, own_ref, pair_ref, core_ref, out_ref, saved_ref, inner_ref, outer_ref):
    parity, core = place_ref[0], place_ref[1]
    pairs = out_ref.shape[0]
    slots = CAP * pairs
    rows = ordered(rows_ref[...], pairs)
    piece = lambda k: rows[k * pairs : k * pairs + slots]
    saved_ref[0] = piece(16).astype(BF16)
    saved_ref[1] = piece(20).astype(BF16)
    low = iota((slots, LANES), 1) < HALF
    turn = lambda x: jnp.where(core == 0, x, pltpu.roll(x, HALF, 1))
    product = 0.0
    for side, mine_ref, out in ((0, own_ref, inner_ref), (1, pair_ref, outer_ref)):
        here = parity == side
        sent = turn(jnp.where(here, piece(0), piece(8)))
        taken = turn(jnp.where(here, piece(4), piece(12)))
        product = product + matmul(sent.astype(BF16), jnp.concatenate([mine_ref[...], core_ref[side]]))
        out[0] = jnp.where(low, sent, pltpu.roll(taken, HALF, 1)).astype(BF16)
        out[1] = jnp.where(low, pltpu.roll(sent, HALF, 1), taken).astype(BF16)
    for k in range(pairs):
        out_ref[k] = product[:, k * LANES : (k + 1) * LANES].astype(BF16)


def hidden_body(parts_ref, saved_ref, out_ref):
    slots = parts_ref.shape[1]
    hidden = jnp.sum(parts_ref[...].astype(F32), axis=0).astype(BF16).astype(F32)
    a, b = saved_ref[0].astype(F32), saved_ref[1].astype(F32)
    q = jax.nn.sigmoid(a)
    out_ref[0, :slots, :] = (hidden * b * q * (1.0 + a * (1.0 - q))).astype(BF16)
    out_ref[0, slots : 2 * slots, :] = (hidden * a * q).astype(BF16)
    out_ref[0, 2 * slots :, :] = (a * q * b).astype(BF16)


def slot_body(place_ref, grads_ref, outer_ref, own_ref, pair_ref, core_ref, out_ref, packed_ref):
    pairs = grads_ref.shape[0]
    packed_ref[: -2 * CAP * pairs, :] = grads_ref[...].reshape(-1, LANES)
    packed_ref[-2 * CAP * pairs :, :] = outer_ref[...].reshape(-1, LANES)
    slots = CAP * pairs
    total = [0.0, 0.0]
    for kind in range(2):
        grads = jnp.concatenate(
            [grads_ref[m, kind * slots : (kind + 1) * slots, :] for m in range(pairs)], axis=1
        )
        for side, mine_ref in enumerate((own_ref, pair_ref)):
            weights = jnp.concatenate([mine_ref[kind], core_ref[side, kind]])
            total[side] = total[side] + matmul(grads, weights, NT)
    row, slot = iota((8 * pairs, slots), 0), iota((8 * pairs, slots), 1)
    placed = 0.0
    for half in range(2):
        place = (slot % pairs == (row // 8) ^ place_ref[2]) & (row % 8 == 4 * half + slot // pairs)
        placed = placed + matmul(place.astype(BF16), total[half].astype(BF16))
    out_ref[...] = placed.astype(BF16).reshape(out_ref.shape)


def join_body(_, own_ref, inner_ref, pair_ref, out_ref):
    slots = inner_ref.shape[1]
    split = own_ref.shape[0]
    out_ref[0, :split, :] = own_ref[...]
    out_ref[0, split:, :] = inner_ref[1]
    out_ref[1, :split, :] = pair_ref[:split, :]
    out_ref[1, split:, :] = pair_ref[split + slots :, :]


def grad_body(inner_ref, own_ref, pair_ref, core_ref, gate_ref, up_ref, down_ref, done_ref):
    slots = inner_ref.shape[1]
    split = own_ref.shape[0]
    lefts = [inner_ref[0], pair_ref[split : split + slots, :], core_ref[0, split:, :], core_ref[1, split:, :]]
    left = jnp.concatenate(lefts).astype(F32).T.astype(BF16)
    sent, taken = left[:HALF], left[HALF:]
    rights = (own_ref, pair_ref, core_ref.at[0], core_ref.at[1])
    for m in range(split // (3 * slots)):
        columns = slice(m * LANES, (m + 1) * LANES)
        for kind, (rows, out_ref) in enumerate(((taken, gate_ref), (taken, up_ref), (sent, down_ref))):
            start = (3 * m + kind) * slots
            right = jnp.concatenate([ref[start : start + slots, :] for ref in rights])
            out_ref[:, columns] = matmul(rows, right)
    done_ref[...] = jnp.zeros_like(done_ref)


def token_body(place_ref, _, index_ref, rows_ref, out_ref):
    parity, core = place_ref[0], place_ref[1]
    tokens = iota((out_ref.shape[0], index_ref.shape[1]), 0)
    sides = []
    for side in range(2):
        owner = (tokens == index_ref[side : side + 1, :]).astype(BF16)
        total = matmul(owner, rows_ref[...])
        sides.append(jnp.where(core == 0, total, pltpu.roll(total, HALF, 1)))
    near, far = sides
    out_ref[:, :LANES] = jnp.where(parity == 0, near, far).astype(BF16)
    out_ref[:, LANES:] = jnp.where(parity == 0, far, near).astype(BF16)


def swap(x, axis):
    return lax.ppermute(x, axis, [(0, 1), (1, 0)])


def transpose(x, pairs):
    moves = [(m * pairs + f, (m ^ f) * pairs + m) for m in range(pairs) for f in range(pairs)]
    return lax.ppermute(x, ("m", "expert"), moves)


def spread(x, axis):
    return lax.all_to_all(x, axis, split_axis=0, concat_axis=0, tiled=True)


def local(pairs, tokens, grad_out, picked, pick_counts, router_weights, saved_gate, saved_up, w_gate, w_up, w_down):
    experts = picked.shape[1]
    token_count, width = tokens.shape
    hidden = w_gate.shape[2]
    slots = CAP * pairs
    place = jnp.stack([lax.axis_index("p"), lax.axis_index("core"), lax.axis_index("m")]).astype(jnp.int32)

    outgoing = call(
        pick_body,
        struct(experts, 8, width),
        [FETCH] * 5,
        scratch=(pltpu.VMEM((width // LANES, 8 * experts, LANES), F32),),
        limit=60,
    )(picked.transpose(2, 0, 1), pick_counts, router_weights.transpose(2, 0, 1), tokens, grad_out)
    saved = call(saved_body, struct(pairs, 8, LANES), [VMEM] * 2)(saved_gate[0], saved_up[0])
    blocks = spread(outgoing, "expert")

    down = w_down[0].T
    down_pair = swap(down, "p")
    down_core = swap(jnp.stack([down, down_pair]), "core")
    own = jnp.stack([w_gate[0], w_up[0]])
    pair = swap(own, "p")
    core = swap(jnp.stack([own, pair]), "core")

    rows = call(send_body, struct(pairs, 24, LANES), [VMEM] * 2)(blocks, saved)
    rows = spread(rows, "m")
    parts, saved, inner, outer = call(
        partial_body,
        (struct(pairs, slots, LANES),) + (struct(2, slots, LANES),) * 3,
        [SMEM] + [VMEM] * 4,
    )(place, rows.reshape(24 * pairs, LANES), down, down_pair, down_core)

    parts = spread(parts, "m")
    grads = call(hidden_body, struct(1, 3 * slots, LANES), [VMEM] * 2)(parts, saved)
    grads = lax.all_gather(grads, "m", axis=0, tiled=True)
    flat = grads.reshape(3 * slots * pairs, LANES)
    packed_rows = 3 * slots * pairs + 2 * slots
    back, packed = call(
        slot_body, (struct(pairs, 8, LANES), struct(packed_rows, LANES)), [SMEM] + [VMEM] * 5
    )(place, grads, outer, own, pair, core)
    packed_pair = swap(packed, "p")
    back = spread(back, "expert")
    packed_core = call(join_body, struct(2, packed_rows - slots, LANES), [ANY] + [VMEM] * 3)(
        back, flat, inner, packed_pair
    )
    packed_core = swap(packed_core, "core")
    back = transpose(back, pairs)

    gate_grad, up_grad, down_grad, done = call(
        grad_body, (struct(HALF, hidden, dtype=F32),) * 3 + (struct(8, LANES, dtype=F32),), [VMEM] * 4
    )(inner, flat, packed_pair, packed_core)

    index = jnp.pad(picked[0], ((0, 0), (0, 1)), constant_values=-1)
    index = jnp.tile(index, (1, 2)).reshape(1, -1)
    upper = jnp.arange(8 * experts, dtype=jnp.int32)[None, :] // 4 % 2
    index = jnp.where(upper == jnp.arange(2)[:, None], index, -1)
    token_grad = call(token_body, struct(token_count, width), [SMEM] + [VMEM] * 3)(
        place, done, index, back.reshape(8 * experts, LANES)
    )
    return (token_grad, gate_grad[None], up_grad[None], down_grad.T[None])


def solution(mesh):
    pairs = mesh.shape["dp"] // 4
    fine = Mesh(mesh.devices.reshape(pairs, 2, 2, mesh.shape["expert"]), ("m", "p", "core", "expert"))
    dp = ("m", "p", "core")
    placed = (
        P(dp, "expert"),
        P(dp, "expert"),
        P(dp, None, None),
        P(dp, None),
        P(dp, None, None),
        P("expert", dp, None),
        P("expert", dp, None),
        P("expert", dp, None),
        P("expert", dp, None),
        P("expert", None, dp),
    )
    return jax.shard_map(
        functools.partial(local, pairs),
        mesh=fine,
        in_specs=placed,
        out_specs=(
            P(dp, "expert"),
            P("expert", dp, None),
            P("expert", dp, None),
            P("expert", None, dp),
        ),
        check_vma=False,
    )
```

```python
import functools

import jax
import jax.numpy as jnp
from jax import lax
from jax.experimental import pallas as pl
from jax.experimental.pallas import tpu as pltpu
from jax.sharding import Mesh
from jax.sharding import PartitionSpec as P

BF16 = jnp.bfloat16
F32 = jnp.float32
CAP = 3
HALF = 64
LANES = 128
NT = (((1,), (1,)), ((), ()))
TN = (((0,), (0,)), ((), ()))
VMEM = pl.BlockSpec(memory_space=pltpu.VMEM)
ANY = pl.BlockSpec(memory_space=pl.ANY)
FETCH = pl.BlockSpec()


def call(body, outs, ins, out_specs=None, scratch=(), limit=24):
    return pl.pallas_call(
        body,
        out_shape=outs,
        in_specs=ins,
        out_specs=jax.tree.map(lambda _: VMEM, outs) if out_specs is None else out_specs,
        scratch_shapes=list(scratch),
        compiler_params=pltpu.CompilerParams(vmem_limit_bytes=limit * 1024 * 1024),
    )


def struct(*shape, dtype=BF16):
    return jax.ShapeDtypeStruct(shape, dtype)


def iota(shape, dim):
    return lax.broadcasted_iota(jnp.int32, shape, dim)


def matmul(left, right, dims=(((1,), (0,)), ((), ()))):
    return lax.dot_general(left, right, dims, preferred_element_type=F32)


def ordered(x, groups):
    total = x.shape[0]
    each = total // groups
    row, column = iota((total, total), 0), iota((total, total), 1)
    order = (row % groups == column // each) & (row // groups == column % each)
    return matmul(order.astype(BF16), x)


def saved_body(gate_ref, up_ref, out_ref):
    blank = jnp.zeros((4 - CAP, LANES), F32)
    for k in range(out_ref.shape[0]):
        columns = slice(k * LANES, (k + 1) * LANES)
        parts = [gate_ref[:, columns].astype(F32), blank, up_ref[:, columns].astype(F32), blank]
        out_ref[k] = jnp.concatenate(parts).astype(BF16)


def pick_body(picked_ref, counts_ref, weights_ref, tokens_ref, grads_ref, out_ref, rows):
    experts = out_ref.shape[0]
    diagonal = iota((experts, experts), 0) == iota((experts, experts), 1)
    rows[...] = jnp.zeros_like(rows)
    for c in range(CAP):
        chosen = (iota((tokens_ref.shape[0], experts), 0) == picked_ref[c]).astype(BF16)
        scale = jnp.where(c < counts_ref[...], weights_ref[c], 0.0)
        scale = jnp.sum(jnp.where(diagonal, scale, 0.0), axis=1, keepdims=True)
        sent = matmul(chosen, grads_ref[...], TN) * scale
        taken = matmul(chosen, tokens_ref[...], TN)
        for row, value in ((c, sent), (4 + c, taken)):
            for j in range(rows.shape[0]):
                rows[j, pl.ds(row, experts, stride=8), :] = value[:, j * LANES : (j + 1) * LANES]
    for j in range(rows.shape[0]):
        out_ref[:, :, j * LANES : (j + 1) * LANES] = rows[j].reshape(experts, 8, LANES).astype(BF16)


def send_body(blocks_ref, saved_ref, out_ref):
    for j in range(2):
        out_ref[:, 8 * j : 8 * j + 8, :] = blocks_ref[:, :, j * LANES : (j + 1) * LANES]
    out_ref[:, 16:, :] = saved_ref[...]


def partial_body(rows_ref, own_ref, pair_ref, core_ref, out_ref, saved_ref, inner_ref, outer_ref):
    parity, core = lax.axis_index("p"), lax.axis_index("core")
    pairs = out_ref.shape[0]
    slots = CAP * pairs
    rows = ordered(rows_ref[...], pairs)
    piece = lambda k: rows[k * pairs : k * pairs + slots]
    saved_ref[0] = piece(16).astype(BF16)
    saved_ref[1] = piece(20).astype(BF16)
    low = iota((slots, LANES), 1) < HALF
    turn = lambda x: jnp.where(core == 0, x, pltpu.roll(x, HALF, 1))
    product = 0.0
    for side, mine_ref, out in ((0, own_ref, inner_ref), (1, pair_ref, outer_ref)):
        here = parity == side
        sent = turn(jnp.where(here, piece(0), piece(8)))
        taken = turn(jnp.where(here, piece(4), piece(12)))
        product = product + matmul(sent.astype(BF16), jnp.concatenate([mine_ref[...], core_ref[side]]))
        out[0] = jnp.where(low, sent, pltpu.roll(taken, HALF, 1)).astype(BF16)
        out[1] = jnp.where(low, pltpu.roll(sent, HALF, 1), taken).astype(BF16)
    for k in range(pairs):
        out_ref[k] = product[:, k * LANES : (k + 1) * LANES].astype(BF16)


def hidden_body(parts_ref, saved_ref, out_ref):
    slots = parts_ref.shape[1]
    hidden = jnp.sum(parts_ref[...].astype(F32), axis=0).astype(BF16).astype(F32)
    a, b = saved_ref[0].astype(F32), saved_ref[1].astype(F32)
    q = jax.nn.sigmoid(a)
    out_ref[0, :slots, :] = (hidden * b * q * (1.0 + a * (1.0 - q))).astype(BF16)
    out_ref[0, slots : 2 * slots, :] = (hidden * a * q).astype(BF16)
    out_ref[0, 2 * slots :, :] = (a * q * b).astype(BF16)


def slot_body(grads_ref, outer_ref, own_ref, pair_ref, core_ref, out_ref, packed_ref):
    pairs = grads_ref.shape[0]
    packed_ref[: -2 * CAP * pairs, :] = grads_ref[...].reshape(-1, LANES)
    packed_ref[-2 * CAP * pairs :, :] = outer_ref[...].reshape(-1, LANES)
    slots = CAP * pairs
    total = [0.0, 0.0]
    for kind in range(2):
        grads = jnp.concatenate(
            [grads_ref[m, kind * slots : (kind + 1) * slots, :] for m in range(pairs)], axis=1
        )
        for side, mine_ref in enumerate((own_ref, pair_ref)):
            weights = jnp.concatenate([mine_ref[kind], core_ref[side, kind]])
            total[side] = total[side] + matmul(grads, weights, NT)
    row, slot = iota((8 * pairs, slots), 0), iota((8 * pairs, slots), 1)
    placed = 0.0
    for half in range(2):
        place = (slot % pairs == (row // 8) ^ lax.axis_index("m")) & (row % 8 == 4 * half + slot // pairs)
        placed = placed + matmul(place.astype(BF16), total[half].astype(BF16))
    out_ref[...] = placed.astype(BF16).reshape(out_ref.shape)


def join_body(_, own_ref, inner_ref, pair_ref, out_ref):
    slots = inner_ref.shape[1]
    split = own_ref.shape[0]
    out_ref[0, :split, :] = own_ref[...]
    out_ref[0, split:, :] = inner_ref[1]
    out_ref[1, :split, :] = pair_ref[:split, :]
    out_ref[1, split:, :] = pair_ref[split + slots :, :]


def grad_body(inner_ref, own_ref, pair_ref, core_ref, gate_ref, up_ref, down_ref, done_ref):
    slots = inner_ref.shape[1]
    split = own_ref.shape[0]
    lefts = [inner_ref[0], pair_ref[split : split + slots, :], core_ref[0, split:, :], core_ref[1, split:, :]]
    left = jnp.concatenate(lefts).astype(F32).T.astype(BF16)
    sent, taken = left[:HALF], left[HALF:]
    rights = (own_ref, pair_ref, core_ref.at[0], core_ref.at[1])
    for m in range(split // (3 * slots)):
        columns = slice(m * LANES, (m + 1) * LANES)
        for kind, (rows, out_ref) in enumerate(((taken, gate_ref), (taken, up_ref), (sent, down_ref))):
            start = (3 * m + kind) * slots
            right = jnp.concatenate([ref[start : start + slots, :] for ref in rights])
            out_ref[:, columns] = matmul(rows, right)
    done_ref[...] = jnp.zeros_like(done_ref)


def token_body(_, index_ref, rows_ref, out_ref):
    parity, core = lax.axis_index("p"), lax.axis_index("core")
    tokens = iota((out_ref.shape[0], index_ref.shape[1]), 0)
    sides = []
    for side in range(2):
        owner = (tokens == index_ref[side : side + 1, :]).astype(BF16)
        total = matmul(owner, rows_ref[...])
        sides.append(jnp.where(core == 0, total, pltpu.roll(total, HALF, 1)))
    near, far = sides
    out_ref[:, :LANES] = jnp.where(parity == 0, near, far).astype(BF16)
    out_ref[:, LANES:] = jnp.where(parity == 0, far, near).astype(BF16)


def swap(x, axis):
    return lax.ppermute(x, axis, [(0, 1), (1, 0)])


def transpose(x, pairs):
    moves = [(m * pairs + f, (m ^ f) * pairs + m) for m in range(pairs) for f in range(pairs)]
    return lax.ppermute(x, ("m", "expert"), moves)


def spread(x, axis):
    return lax.all_to_all(x, axis, split_axis=0, concat_axis=0, tiled=True)


def local(pairs, tokens, grad_out, picked, pick_counts, router_weights, saved_gate, saved_up, w_gate, w_up, w_down):
    experts = picked.shape[1]
    token_count, width = tokens.shape
    hidden = w_gate.shape[2]
    slots = CAP * pairs

    outgoing = call(
        pick_body,
        struct(experts, 8, width),
        [FETCH] * 5,
        scratch=(pltpu.VMEM((width // LANES, 8 * experts, LANES), F32),),
        limit=60,
    )(picked.transpose(2, 0, 1), pick_counts, router_weights.transpose(2, 0, 1), tokens, grad_out)
    saved = call(saved_body, struct(pairs, 8, LANES), [VMEM] * 2)(saved_gate[0], saved_up[0])
    blocks = spread(outgoing, "expert")

    down = w_down[0].T
    down_pair = swap(down, "p")
    down_core = swap(jnp.stack([down, down_pair]), "core")
    own = jnp.stack([w_gate[0], w_up[0]])
    pair = swap(own, "p")
    core = swap(jnp.stack([own, pair]), "core")

    rows = call(send_body, struct(pairs, 24, LANES), [VMEM] * 2)(blocks, saved)
    rows = spread(rows, "m")
    parts, saved, inner, outer = call(
        partial_body,
        (struct(pairs, slots, LANES),) + (struct(2, slots, LANES),) * 3,
        [VMEM] * 4,
    )(rows.reshape(24 * pairs, LANES), down, down_pair, down_core)

    parts = spread(parts, "m")
    grads = call(hidden_body, struct(1, 3 * slots, LANES), [VMEM] * 2)(parts, saved)
    grads = lax.all_gather(grads, "m", axis=0, tiled=True)
    flat = grads.reshape(3 * slots * pairs, LANES)
    packed_rows = 3 * slots * pairs + 2 * slots
    back, packed = call(
        slot_body, (struct(pairs, 8, LANES), struct(packed_rows, LANES)), [VMEM] * 5
    )(grads, outer, own, pair, core)
    packed_pair = swap(packed, "p")
    back = spread(back, "expert")
    packed_core = call(join_body, struct(2, packed_rows - slots, LANES), [ANY] + [VMEM] * 3)(
        back, flat, inner, packed_pair
    )
    packed_core = swap(packed_core, "core")
    back = transpose(back, pairs)

    gate_grad, up_grad, down_grad, done = call(
        grad_body, (struct(HALF, hidden, dtype=F32),) * 3 + (struct(8, LANES, dtype=F32),), [VMEM] * 4
    )(inner, flat, packed_pair, packed_core)

    index = jnp.pad(picked[0], ((0, 0), (0, 1)), constant_values=-1)
    index = jnp.tile(index, (1, 2)).reshape(1, -1)
    upper = jnp.arange(8 * experts, dtype=jnp.int32)[None, :] // 4 % 2
    index = jnp.where(upper == jnp.arange(2)[:, None], index, -1)
    token_grad = call(token_body, struct(token_count, width), [VMEM] * 3)(
        done, index, back.reshape(8 * experts, LANES)
    )
    return (token_grad, gate_grad[None], up_grad[None], down_grad.T[None])


def solution(mesh):
    pairs = mesh.shape["dp"] // 4
    fine = Mesh(mesh.devices.reshape(pairs, 2, 2, mesh.shape["expert"]), ("m", "p", "core", "expert"))
    dp = ("m", "p", "core")
    placed = (
        P(dp, "expert"),
        P(dp, "expert"),
        P(dp, None, None),
        P(dp, None),
        P(dp, None, None),
        P("expert", dp, None),
        P("expert", dp, None),
        P("expert", dp, None),
        P("expert", dp, None),
        P("expert", None, dp),
    )
    return jax.shard_map(
        functools.partial(local, pairs),
        mesh=fine,
        in_specs=placed,
        out_specs=(
            P(dp, "expert"),
            P("expert", dp, None),
            P("expert", dp, None),
            P("expert", None, dp),
        ),
        check_vma=False,
    )
```
